32 devices in a mesh: occ: 2 (over y), virt: 4 (over z), aux: 4 (over x, core).
Axes of the slice: x: 2, y: 2, z: 4, core: 2. Of those that a mesh axis runs over, the one named last changes fastest.
Arguments:
- factors: bfloat16 [3072, 4, 1024], P('aux', 'occ', 'virt'), may hold values from -2 to 2
- occ_energy: float32 [4], replicated, may hold values from -2 to -0.3
- virt_energy: float32 [1024], replicated, may hold values from 0.2 to 3
Outputs:
- density: float32 [3072, 4, 1024], P('aux', 'occ', 'virt')
The draws below stay inside these ranges and needn't reach their ends.
All inputs are finite; a program needn't handle non-finite values.
Results may differ from the reference program's by a relative error of at most 0.0016.
Values may be sent and summed in bfloat16 or wider, within the bound.
A program may use at most 128 MiB of HBM per device.

```python
import jax
import jax.numpy as jnp
from jax import lax

NAUX = 3072
NVIRT = 1024
OCC_DEV = 2
NOCC = 4
STEPS = 2


def steps_of(rng, shape, shards, smallest, top_value):
    level = 1.0
    for axis_at, blocks in shards:
        steps = jax.random.uniform(jax.random.fold_in(jax.random.fold_in(rng, 6), axis_at), (blocks,), jnp.float32, smallest / len(shards), top_value / len(shards))
        level = level * jnp.repeat(jnp.exp(steps), shape[axis_at] // blocks).reshape((-1,) + (1,) * (len(shape) - 1 - axis_at))
    return level


def normal_values(key, dims, scale, limit, cuts=(), kind=jnp.bfloat16):
    drawn = jax.random.normal(key, dims, jnp.float32) * scale
    if len(cuts) > 0:
        drawn = steps_of(key, dims, cuts, -0.22, 0.18) * drawn
    return jnp.clip(drawn, min=-limit, max=limit).astype(kind)


def setup_inputs(seed: int = 0) -> dict:
    streams_of = jax.random.split(jax.random.key(seed), 4)
    return {
        "factors": normal_values(streams_of[0], (NAUX, NOCC, NVIRT), (NAUX ** -0.25), 2.0, ((0, 4), (1, 2), (2, 4))),
        "occ_energy": jnp.clip(jax.random.uniform(streams_of[1], (NOCC,), jnp.float32, -2.0, -0.3), -2.0, -0.3),
        "virt_energy": jnp.clip(jax.random.uniform(streams_of[2], (NVIRT,), jnp.float32, 0.2, 3.0), 0.2, 3.0),
    }


def reference(factors, occ_energy, virt_energy):
    blocks = NOCC // OCC_DEV
    whole = factors.astype(jnp.float32).reshape(NAUX, blocks, OCC_DEV, NVIRT)
    energy_blocks = occ_energy.reshape(blocks, OCC_DEV)
    density = jnp.zeros((blocks, NAUX, OCC_DEV, NVIRT), jnp.float32)

    def one_block(items):
        local, partner, eo_i, eo_j = items
        ints = jnp.einsum('qia,qjb->iajb', local, partner, precision=lax.Precision.HIGHEST)
        gap = eo_i[:, None, None, None] + eo_j[None, None, :, None] - virt_energy[None, :, None, None] - virt_energy[None, None, None, :]
        amps = lax.optimization_barrier((ints / gap).astype(jnp.bfloat16)).astype(jnp.float32)
        return jnp.einsum('iajb,qjb->qia', amps, partner, precision=lax.Precision.HIGHEST)

    local_all = jnp.moveaxis(whole, 1, 0)
    for step in range(STEPS):
        partner_all = jnp.roll(local_all, step, axis=0)
        partner_energy = jnp.roll(energy_blocks, step, axis=0)
        density = density + lax.map(one_block, (local_all, partner_all, energy_blocks, partner_energy))
    return jnp.moveaxis(density, 0, 1).reshape(NAUX, NOCC, NVIRT)
```

```python
import functools

import jax
import jax.numpy as jnp
from jax import lax
from jax.experimental import pallas as pl
from jax.experimental.pallas import tpu as pltpu
from jax.sharding import PartitionSpec as P

AXES = ("occ", "virt", "aux")
WINDOW = 3
F32, BF16 = jnp.float32, jnp.bfloat16


def nearest(k, v, n):
    left, right = v, n - 1 - v
    short = jnp.minimum(left, right)
    alternating = v - (k + 1) // 2 if k % 2 else v + k // 2
    beyond = jnp.where(left <= right, k, n - 1 - k)
    return jnp.where(k <= 2 * short, alternating, beyond)


def kernel(
    n_occ, n_virt, n_aux, steps,
    f_ref, er_ref, ec_ref, out_ref,
    held, partner, part, sums, amps, dens, dsend, drecv,
    z_send, z_recv, y_send, y_recv, d_send, d_recv, s_send, s_recv, a_send, a_recv,
):
    o, v, u = (lax.axis_index(name) for name in AXES)
    rounds = n_aux.bit_length() - 1
    naux, block = f_ref.shape
    has_left, has_right = v >= 1, v <= n_virt - 2

    def remote(src, dst, send, recv, **where):
        at = {"occ": o, "virt": v, "aux": u, **where}
        return pltpu.make_async_remote_copy(
            src_ref=src, dst_ref=dst, send_sem=send, recv_sem=recv,
            device_id=tuple(at[name] for name in AXES), device_id_type=pl.DeviceIdType.MESH,
        )

    def flip(r):
        bit = 1 << r
        return u + bit - 2 * bit * (u // bit % 2)

    barrier = pltpu.get_barrier_semaphore()

    def greet(**where):
        at = {"occ": o, "virt": v, "aux": u, **where}
        pl.semaphore_signal(
            barrier, inc=1, device_id=tuple(at[name] for name in AXES), device_id_type=pl.DeviceIdType.MESH
        )

    offsets = sorted({d % n_occ for s in range(1, steps) for d in (s, -s)})
    for d in offsets:
        greet(occ=lax.rem(o + d, n_occ))
    for r in range(rounds):
        greet(aux=flip(r))

    @pl.when(has_left)
    def _():
        greet(virt=v - 1)

    @pl.when(has_right)
    def _():
        greet(virt=v + 1)

    ends = jnp.minimum(v, 1) + jnp.minimum(n_virt - 1 - v, 1)
    pl.semaphore_wait(barrier, len(offsets) + rounds + ends)

    def along(src, w, to_right):
        if to_right:
            return remote(src, held.at[w], z_send.at[0, w], z_recv.at[w], virt=v + 1)
        return remote(src, held.at[w], z_send.at[1, w], z_recv.at[w], virt=v - 1)

    @pl.when(has_right)
    def _():
        along(f_ref, v, True).start()

    @pl.when(has_left)
    def _():
        along(f_ref, v, False).start()

    def across(s):
        return remote(
            f_ref, partner.at[s - 1], y_send.at[s - 1], y_recv.at[s - 1], occ=lax.rem(o - s + n_occ, n_occ)
        )

    for s in range(1, steps):
        across(s).start()

    held[pl.ds(v, 1)] = f_ref[...].reshape(1, naux, block)

    def arrive(k):
        @pl.when(v >= k)
        def _():
            w = v - k
            along(held.at[w], w, True).wait_recv()

            @pl.when(has_right)
            def _():
                along(held.at[w], w, True).start()

        @pl.when(v + k <= n_virt - 1)
        def _():
            w = v + k
            along(held.at[w], w, False).wait_recv()

            @pl.when(has_left)
            def _():
                along(held.at[w], w, False).start()

    def size(r):
        return block >> (r + 1)

    def bases(r):
        base = 0
        for t in range(r):
            base = base + (u // (1 << t) % 2) * size(t)
        bit = u // (1 << r) % 2
        keep = pl.multiple_of(base + bit * size(r), size(r))
        give = pl.multiple_of(base + (1 - bit) * size(r), size(r))
        return keep, give

    sum_at = [sum(size(t) for t in range(r)) for r in range(rounds)]

    def sum_copy(p, r):
        _, give = bases(r)
        return remote(
            part.at[p, pl.ds(give, size(r))], sums.at[p, pl.ds(sum_at[r], size(r))],
            s_send.at[p, r], s_recv.at[p, r], aux=flip(r),
        )

    def amp_copy(p, r):
        keep, _ = bases(r)
        rows = pl.ds(keep, size(r))
        return remote(amps.at[p, rows], amps.at[p, rows], a_send.at[p, r], a_recv.at[p, r], aux=flip(r))

    def left_block(k):
        return held[pl.ds(nearest(k, v, n_virt), 1)].reshape(naux, block)

    def integrals(p, k, s):
        cols = f_ref[...] if s == 0 else partner[s - 1]
        part[p] = lax.dot_general(left_block(k), cols, (((0,), (0,)), ((), ())), preferred_element_type=F32)
        sum_copy(p, 0).start()

    def add(p, r):
        keep, _ = bases(r)
        sum_copy(p, r).wait_recv()
        rows = pl.ds(keep, size(r))
        part[p, rows] = part[p, rows] + sums[p, pl.ds(sum_at[r], size(r))]
        if r + 1 < rounds:
            sum_copy(p, r + 1).start()

    def amplitudes(p, k, s):
        keep, _ = bases(rounds - 1)
        rows = pl.ds(keep, size(rounds - 1))
        gap = er_ref[pl.ds(nearest(k, v, n_virt), 1)].reshape(size(rounds - 1), 1) + ec_ref[s : s + 1]
        amps[p, rows] = (part[p, rows] / gap).astype(BF16)
        amp_copy(p, rounds - 1).start()

    def spread(p, r):
        amp_copy(p, r).wait_recv()
        if r > 0:
            amp_copy(p, r - 1).start()

    def contract(p, k, s):
        term = lax.dot_general(left_block(k), amps[p], (((1,), (0,)), ((), ())), preferred_element_type=F32)
        if k == 0:
            dens[s] = term
        else:
            dens[s] = dens[s] + term

    def back(s):
        return remote(
            dsend.at[s - 1], drecv.at[s - 1], d_send.at[s - 1], d_recv.at[s - 1], occ=lax.rem(o + s, n_occ)
        )

    groups = [[(0, 0)]]
    groups.append([(0, s) for s in range(1, steps)])
    for k in range(1, n_virt):
        pieces = [(k, s) for s in reversed(range(steps))]
        if k == 1:
            groups[1] += pieces
        else:
            groups.append(pieces)

    number = 0
    for g, group in enumerate(groups):
        if g > 0:
            arrive(g)
        if g == 1:
            for s in range(1, steps):
                across(s).wait_recv()
        named = []
        for k, s in group:
            named.append((number, k, s))
            number += 1
        for p, k, s in named:
            integrals(p, k, s)
        for r in range(rounds):
            for p, k, s in named:
                add(p, r)
                if r == rounds - 1:
                    amplitudes(p, k, s)
        for p, k, s in named:
            for r in reversed(range(rounds)):
                spread(p, r)
            contract(p, k, s)
            if k == n_virt - 1 and s > 0:
                dsend[s - 1] = dens[s].astype(BF16)
                back(s).start()

    out_ref[...] = dens[0]
    for s in range(1, steps):
        back(s).wait_recv()
        out_ref[...] += drecv[s - 1].astype(F32)

    for s in range(1, steps):
        back(s).wait_send()
        across(s).wait_send()
    for p in range(number):
        for r in range(rounds):
            sum_copy(p, r).wait_send()
            amp_copy(p, r).wait_send()
    for k in range(n_virt - 1):

        @pl.when((v >= k) & has_right)
        def _():
            along(held.at[v - k], v - k, True).wait_send()

        @pl.when((v + k <= n_virt - 1) & has_left)
        def _():
            along(held.at[v + k], v + k, False).wait_send()


def on_device(sizes, factors, occ_energy, virt_energy):
    n_occ, n_virt, n_aux = sizes
    steps = min(WINDOW, n_occ)
    naux, occ_width, virt_width = factors.shape
    block = occ_width * virt_width
    rounds = n_aux.bit_length() - 1
    rows = block // n_aux
    o, v, u = (lax.axis_index(name) for name in AXES)

    eo = occ_energy.reshape(n_occ, occ_width)
    ev = virt_energy.reshape(n_virt, virt_width)
    eo_own = lax.dynamic_index_in_dim(eo, o, 0, keepdims=False)
    er = (eo_own[None, :, None] - ev[:, None, :]).reshape(n_virt, block)
    first = 0
    for r in range(rounds):
        first = first + ((u >> r) & 1) * (block >> (r + 1))
    er = lax.dynamic_slice_in_dim(er, first, rows, 1).reshape(n_virt, rows, 1)
    ev_own = lax.dynamic_index_in_dim(ev, v, 0, keepdims=False)
    eo_cols = jnp.roll(eo, -o, 0)[:steps]
    ec = (eo_cols[:, :, None] - ev_own[None, None, :]).reshape(steps, block)

    pieces = n_virt * steps
    dma = pltpu.SemaphoreType.DMA
    flops = 4 * pieces * naux * block * block
    density = pl.pallas_call(
        functools.partial(kernel, n_occ, n_virt, n_aux, steps),
        out_shape=jax.ShapeDtypeStruct((naux, block), F32),
        in_specs=[pl.BlockSpec(memory_space=pltpu.VMEM)] * 3,
        out_specs=pl.BlockSpec(memory_space=pltpu.VMEM),
        scratch_shapes=[
            pltpu.VMEM((n_virt, naux, block), BF16),
            pltpu.VMEM((steps - 1, naux, block), BF16),
            pltpu.VMEM((pieces, block, block), F32),
            pltpu.VMEM((pieces, block - rows, block), F32),
            pltpu.VMEM((pieces, block, block), BF16),
            pltpu.VMEM((steps, naux, block), F32),
            pltpu.VMEM((steps - 1, naux, block), BF16),
            pltpu.VMEM((steps - 1, naux, block), BF16),
            dma((2, n_virt)), dma((n_virt,)),
            dma((steps - 1,)), dma((steps - 1,)),
            dma((steps - 1,)), dma((steps - 1,)),
            dma((pieces, rounds)), dma((pieces, rounds)),
            dma((pieces, rounds)), dma((pieces, rounds)),
        ],
        compiler_params=pltpu.CompilerParams(
            collective_id=0, has_side_effects=True, vmem_limit_bytes=60 << 20
        ),
        cost_estimate=pl.CostEstimate(flops=flops, bytes_accessed=6 * naux * block, transcendentals=0),
    )(factors.reshape(naux, block), er, ec)
    return density.reshape(factors.shape)


def solution(mesh):
    sizes = tuple(mesh.shape[name] for name in AXES)
    return jax.shard_map(
        functools.partial(on_device, sizes),
        mesh=mesh,
        in_specs=(P("aux", "occ", "virt"), P(), P()),
        out_specs=P("aux", "occ", "virt"),
        check_vma=False,
    )
```

```python
import functools

import jax
import jax.numpy as jnp
from jax import lax
from jax.experimental import pallas as pl
from jax.experimental.pallas import tpu as pltpu
from jax.sharding import PartitionSpec as P

AXES = ("occ", "virt", "aux")
WINDOW = 3
HALVES = 2
SPAN = 120.0
F32, BF16 = jnp.float32, jnp.bfloat16


def nearest(k, v, n):
    left, right = v, n - 1 - v
    short = jnp.minimum(left, right)
    alternating = v - (k + 1) // 2 if k % 2 else v + k // 2
    beyond = jnp.where(left <= right, k, n - 1 - k)
    return jnp.where(k <= 2 * short, alternating, beyond)


def encode(x, top):
    z = jnp.exp2(jnp.abs(x) * (2 * SPAN / top) - SPAN)
    return jnp.where(x < 0, -z, z).astype(BF16)


def decode(z, top):
    z = z.astype(F32)
    x = (jnp.log2(jnp.abs(z)) + SPAN) * (top * (0.5 / SPAN))
    return jnp.where(z < 0, -x, x)


def kernel(
    n_occ, n_virt, n_aux, steps,
    f_ref, er_ref, ec_ref, out_ref,
    held, partner, part, sums, code_out, code_in, top_out, top_in, amps, dens, dsend, drecv,
    z_send, z_recv, y_send, y_recv, d_send, d_recv, s_send, s_recv, t_send, t_recv, a_send, a_recv,
):
    o, v, u = (lax.axis_index(name) for name in AXES)
    rounds = n_aux.bit_length() - 1
    naux, block = f_ref.shape
    has_left, has_right = v >= 1, v <= n_virt - 2

    def remote(src, dst, send, recv, **where):
        at = {"occ": o, "virt": v, "aux": u, **where}
        return pltpu.make_async_remote_copy(
            src_ref=src, dst_ref=dst, send_sem=send, recv_sem=recv,
            device_id=tuple(at[name] for name in AXES), device_id_type=pl.DeviceIdType.MESH,
        )

    def flip(r):
        bit = 1 << r
        return u + bit - 2 * bit * (u // bit % 2)

    barrier = pltpu.get_barrier_semaphore()

    def greet(**where):
        at = {"occ": o, "virt": v, "aux": u, **where}
        pl.semaphore_signal(
            barrier, inc=1, device_id=tuple(at[name] for name in AXES), device_id_type=pl.DeviceIdType.MESH
        )

    offsets = sorted({d % n_occ for s in range(1, steps) for d in (s, -s)})
    for d in offsets:
        greet(occ=lax.rem(o + d, n_occ))
    for r in range(rounds):
        greet(aux=flip(r))

    @pl.when(has_left)
    def _():
        greet(virt=v - 1)

    @pl.when(has_right)
    def _():
        greet(virt=v + 1)

    ends = jnp.minimum(v, 1) + jnp.minimum(n_virt - 1 - v, 1)
    pl.semaphore_wait(barrier, len(offsets) + rounds + ends)

    deep = naux // HALVES

    def along(src, w, h, to_right):
        rows = pl.ds(h * deep, deep)
        if to_right:
            return remote(src.at[rows], held.at[w, rows], z_send.at[0, w, h], z_recv.at[w, h], virt=v + 1)
        return remote(src.at[rows], held.at[w, rows], z_send.at[1, w, h], z_recv.at[w, h], virt=v - 1)

    @pl.when(has_right)
    def _():
        for h in range(HALVES):
            along(f_ref, v, h, True).start()

    @pl.when(has_left)
    def _():
        for h in range(HALVES):
            along(f_ref, v, h, False).start()

    def across(s):
        return remote(
            f_ref, partner.at[s - 1], y_send.at[s - 1], y_recv.at[s - 1], occ=lax.rem(o - s + n_occ, n_occ)
        )

    for s in range(1, steps):
        across(s).start()

    held[pl.ds(v, 1)] = f_ref[...].reshape(1, naux, block)

    def arrive(k, h):
        @pl.when(v >= k)
        def _():
            w = v - k
            along(held.at[w], w, h, True).wait_recv()

            @pl.when(has_right)
            def _():
                along(held.at[w], w, h, True).start()

        @pl.when(v + k <= n_virt - 1)
        def _():
            w = v + k
            along(held.at[w], w, h, False).wait_recv()

            @pl.when(has_left)
            def _():
                along(held.at[w], w, h, False).start()

    def size(r):
        return block >> (r + 1)

    def bases(r):
        base = 0
        for t in range(r):
            base = base + (u // (1 << t) % 2) * size(t)
        bit = u // (1 << r) % 2
        keep = pl.multiple_of(base + bit * size(r), size(r))
        give = pl.multiple_of(base + (1 - bit) * size(r), size(r))
        return keep, give

    code_at = [0] + [sum(size(t) for t in range(1, r)) for r in range(1, rounds)]

    def sum_copy(p, r):
        if r == 0:
            src, dst = part.at[p, pl.ds(bases(0)[1], size(0))], sums.at[p]
        else:
            rows = pl.ds(code_at[r], size(r))
            src, dst = code_out.at[p, rows], code_in.at[p, rows]
        return remote(src, dst, s_send.at[p, r], s_recv.at[p, r], aux=flip(r))

    def top_copy(p, r):
        return remote(top_out.at[p, r], top_in.at[p, r], t_send.at[p, r], t_recv.at[p, r], aux=flip(r))

    def amp_copy(p, r):
        keep, _ = bases(r)
        rows = pl.ds(keep, size(r))
        return remote(amps.at[p, rows], amps.at[p, rows], a_send.at[p, r], a_recv.at[p, r], aux=flip(r))

    def left_block(k):
        return held[pl.ds(nearest(k, v, n_virt), 1)].reshape(naux, block)

    def integrals(p, k, s):
        cols = f_ref[...] if s == 0 else partner[s - 1]
        part[p] = lax.dot_general(left_block(k), cols, (((0,), (0,)), ((), ())), preferred_element_type=F32)
        sum_copy(p, 0).start()

    def add(p, r):
        keep, _ = bases(r)
        sum_copy(p, r).wait_recv()
        rows = pl.ds(keep, size(r))
        if r == 0:
            part[p, rows] = part[p, rows] + sums[p]
        else:
            top_copy(p, r).wait_recv()
            part[p, rows] = part[p, rows] + decode(code_in[p, pl.ds(code_at[r], size(r))], top_in[p, r, :1, :1])
        if r + 1 < rounds:
            _, give = bases(r + 1)
            x = part[p, pl.ds(give, size(r + 1))]
            top = jnp.maximum(jnp.max(jnp.abs(x), axis=(0, 1), keepdims=True), 1e-30)
            top_out[p, r + 1] = jnp.broadcast_to(top, top_out.shape[2:])
            code_out[p, pl.ds(code_at[r + 1], size(r + 1))] = encode(x, top)
            top_copy(p, r + 1).start()
            sum_copy(p, r + 1).start()

    def amplitudes(p, k, s):
        keep, _ = bases(rounds - 1)
        rows = pl.ds(keep, size(rounds - 1))
        gap = er_ref[pl.ds(nearest(k, v, n_virt), 1)].reshape(size(rounds - 1), 1) + ec_ref[s : s + 1]
        amps[p, rows] = (part[p, rows] / gap).astype(BF16)
        amp_copy(p, rounds - 1).start()

    def spread(p, r):
        amp_copy(p, r).wait_recv()
        if r > 0:
            amp_copy(p, r - 1).start()

    def contract(p, k, s):
        term = lax.dot_general(left_block(k), amps[p], (((1,), (0,)), ((), ())), preferred_element_type=F32)
        if k == 0:
            dens[s] = term
        else:
            dens[s] = dens[s] + term

    def back(s):
        return remote(
            dsend.at[s - 1], drecv.at[s - 1], d_send.at[s - 1], d_recv.at[s - 1], occ=lax.rem(o + s, n_occ)
        )

    groups = [[(0, 0)]]
    groups.append([(0, s) for s in range(1, steps)])
    for k in range(1, n_virt):
        pieces = [(k, s) for s in reversed(range(steps))]
        if k == 1:
            groups[1] += pieces
        else:
            groups.append(pieces)

    def finish(p, k, s):
        for r in reversed(range(rounds)):
            spread(p, r)
        contract(p, k, s)
        if k == n_virt - 1 and s > 0:
            dsend[s - 1] = dens[s].astype(BF16)
            back(s).start()

    number = 0
    for g, group in enumerate(groups):
        if g > 0:
            for h in range(HALVES):
                arrive(g, h)
        if g == 1:
            for s in range(1, steps):
                across(s).wait_recv()
        named = []
        for k, s in group:
            named.append((number, k, s))
            number += 1
        for p, k, s in named:
            integrals(p, k, s)
        last = g == len(groups) - 1
        for r in range(rounds):
            for p, k, s in named:
                add(p, r)
                if r == rounds - 1:
                    amplitudes(p, k, s)
                    if last:
                        finish(p, k, s)
        if not last:
            for p, k, s in named:
                finish(p, k, s)

    out_ref[...] = dens[0]
    for s in range(1, steps):
        back(s).wait_recv()
        out_ref[...] += drecv[s - 1].astype(F32)

    for s in range(1, steps):
        back(s).wait_send()
        across(s).wait_send()
    for p in range(number):
        for r in range(rounds):
            sum_copy(p, r).wait_send()
            if r > 0:
                top_copy(p, r).wait_send()
            amp_copy(p, r).wait_send()
    for k in range(n_virt - 1):

        @pl.when((v >= k) & has_right)
        def _():
            for h in range(HALVES):
                along(held.at[v - k], v - k, h, True).wait_send()

        @pl.when((v + k <= n_virt - 1) & has_left)
        def _():
            for h in range(HALVES):
                along(held.at[v + k], v + k, h, False).wait_send()


def on_device(sizes, factors, occ_energy, virt_energy):
    n_occ, n_virt, n_aux = sizes
    steps = min(WINDOW, n_occ)
    naux, occ_width, virt_width = factors.shape
    block = occ_width * virt_width
    rounds = n_aux.bit_length() - 1
    rows = block // n_aux
    o, v, u = (lax.axis_index(name) for name in AXES)

    eo = occ_energy.reshape(n_occ, occ_width)
    ev = virt_energy.reshape(n_virt, virt_width)
    eo_own = lax.dynamic_index_in_dim(eo, o, 0, keepdims=False)
    er = (eo_own[None, :, None] - ev[:, None, :]).reshape(n_virt, block)
    first = 0
    for r in range(rounds):
        first = first + ((u >> r) & 1) * (block >> (r + 1))
    er = lax.dynamic_slice_in_dim(er, first, rows, 1).reshape(n_virt, rows, 1)
    ev_own = lax.dynamic_index_in_dim(ev, v, 0, keepdims=False)
    eo_cols = jnp.roll(eo, -o, 0)[:steps]
    ec = (eo_cols[:, :, None] - ev_own[None, None, :]).reshape(steps, block)

    pieces = n_virt * steps
    dma = pltpu.SemaphoreType.DMA
    flops = 4 * pieces * naux * block * block
    density = pl.pallas_call(
        functools.partial(kernel, n_occ, n_virt, n_aux, steps),
        out_shape=jax.ShapeDtypeStruct((naux, block), F32),
        in_specs=[pl.BlockSpec(memory_space=pltpu.VMEM)] * 3,
        out_specs=pl.BlockSpec(memory_space=pltpu.VMEM),
        scratch_shapes=[
            pltpu.VMEM((n_virt, naux, block), BF16),
            pltpu.VMEM((steps - 1, naux, block), BF16),
            pltpu.VMEM((pieces, block, block), F32),
            pltpu.VMEM((pieces, block // 2, block), F32),
            pltpu.VMEM((pieces, block // 2 - rows, block), BF16),
            pltpu.VMEM((pieces, block // 2 - rows, block), BF16),
            pltpu.VMEM((pieces, rounds, 8, 128), F32),
            pltpu.VMEM((pieces, rounds, 8, 128), F32),
            pltpu.VMEM((pieces, block, block), BF16),
            pltpu.VMEM((steps, naux, block), F32),
            pltpu.VMEM((steps - 1, naux, block), BF16),
            pltpu.VMEM((steps - 1, naux, block), BF16),
            dma((2, n_virt, HALVES)), dma((n_virt, HALVES)),
            dma((steps - 1,)), dma((steps - 1,)),
            dma((steps - 1,)), dma((steps - 1,)),
            dma((pieces, rounds)), dma((pieces, rounds)),
            dma((pieces, rounds)), dma((pieces, rounds)),
            dma((pieces, rounds)), dma((pieces, rounds)),
        ],
        compiler_params=pltpu.CompilerParams(
            collective_id=0, has_side_effects=True, vmem_limit_bytes=60 << 20
        ),
        cost_estimate=pl.CostEstimate(flops=flops, bytes_accessed=6 * naux * block, transcendentals=0),
    )(factors.reshape(naux, block), er, ec)
    return density.reshape(factors.shape)


def solution(mesh):
    sizes = tuple(mesh.shape[name] for name in AXES)
    return jax.shard_map(
        functools.partial(on_device, sizes),
        mesh=mesh,
        in_specs=(P("aux", "occ", "virt"), P(), P()),
        out_specs=P("aux", "occ", "virt"),
        check_vma=False,
    )
```

```python
import functools

import jax
import jax.numpy as jnp
from jax import lax
from jax.experimental import pallas as pl
from jax.experimental.pallas import tpu as pltpu
from jax.sharding import PartitionSpec as P

AXES = ("occ", "virt", "aux")
WINDOW = 3
HALVES = 2
SPAN = 120.0
F32, BF16 = jnp.float32, jnp.bfloat16


def nearest(k, v, n):
    left, right = v, n - 1 - v
    short = jnp.minimum(left, right)
    alternating = v - (k + 1) // 2 if k % 2 else v + k // 2
    beyond = jnp.where(left <= right, k, n - 1 - k)
    return jnp.where(k <= 2 * short, alternating, beyond)


def encode(x, top):
    z = jnp.exp2(jnp.abs(x) * (2 * SPAN / top) - SPAN)
    return jnp.where(x < 0, -z, z).astype(BF16)


def decode(z, top):
    z = z.astype(F32)
    x = (jnp.log2(jnp.abs(z)) + SPAN) * (top * (0.5 / SPAN))
    return jnp.where(z < 0, -x, x)


def kernel(
    n_occ, n_virt, n_aux, steps,
    f_ref, er_ref, ec_ref, out_ref,
    held, partner, part, sums, code_out, code_in, top_out, top_in, amps, dens, dsend, drecv,
    z_send, z_recv, y_send, y_recv, d_send, d_recv, s_send, s_recv, t_send, t_recv, a_send, a_recv,
):
    o, v, u = (lax.axis_index(name) for name in AXES)
    rounds = n_aux.bit_length() - 1
    naux, block = f_ref.shape
    has_left, has_right = v >= 1, v <= n_virt - 2

    def remote(src, dst, send, recv, **where):
        at = {"occ": o, "virt": v, "aux": u, **where}
        return pltpu.make_async_remote_copy(
            src_ref=src, dst_ref=dst, send_sem=send, recv_sem=recv,
            device_id=tuple(at[name] for name in AXES), device_id_type=pl.DeviceIdType.MESH,
        )

    def flip(r):
        bit = 1 << r
        return u + bit - 2 * bit * (u // bit % 2)

    barrier = pltpu.get_barrier_semaphore()

    def greet(**where):
        at = {"occ": o, "virt": v, "aux": u, **where}
        pl.semaphore_signal(
            barrier, inc=1, device_id=tuple(at[name] for name in AXES), device_id_type=pl.DeviceIdType.MESH
        )

    offsets = sorted({d % n_occ for s in range(1, steps) for d in (s, -s)})
    for d in offsets:
        greet(occ=lax.rem(o + d, n_occ))
    for r in range(rounds):
        greet(aux=flip(r))

    @pl.when(has_left)
    def _():
        greet(virt=v - 1)

    @pl.when(has_right)
    def _():
        greet(virt=v + 1)

    ends = jnp.minimum(v, 1) + jnp.minimum(n_virt - 1 - v, 1)
    pl.semaphore_wait(barrier, len(offsets) + rounds + ends)

    deep = naux // HALVES

    def along(src, w, h, to_right):
        rows = pl.ds(h * deep, deep)
        if to_right:
            return remote(src.at[rows], held.at[w, rows], z_send.at[0, w, h], z_recv.at[w, h], virt=v + 1)
        return remote(src.at[rows], held.at[w, rows], z_send.at[1, w, h], z_recv.at[w, h], virt=v - 1)

    @pl.when(has_right)
    def _():
        for h in range(HALVES):
            along(f_ref, v, h, True).start()

    @pl.when(has_left)
    def _():
        for h in range(HALVES):
            along(f_ref, v, h, False).start()

    def across(s):
        return remote(
            f_ref, partner.at[s - 1], y_send.at[s - 1], y_recv.at[s - 1], occ=lax.rem(o - s + n_occ, n_occ)
        )

    for s in range(1, steps):
        across(s).start()

    held[pl.ds(v, 1)] = f_ref[...].reshape(1, naux, block)

    def arrive(k, h):
        @pl.when(v >= k)
        def _():
            w = v - k
            along(held.at[w], w, h, True).wait_recv()

            @pl.when(has_right)
            def _():
                along(held.at[w], w, h, True).start()

        @pl.when(v + k <= n_virt - 1)
        def _():
            w = v + k
            along(held.at[w], w, h, False).wait_recv()

            @pl.when(has_left)
            def _():
                along(held.at[w], w, h, False).start()

    def size(r):
        return block >> (r + 1)

    def bases(r):
        base = 0
        for t in range(r):
            base = base + (u // (1 << t) % 2) * size(t)
        bit = u // (1 << r) % 2
        keep = pl.multiple_of(base + bit * size(r), size(r))
        give = pl.multiple_of(base + (1 - bit) * size(r), size(r))
        return keep, give

    code_at = [0] + [sum(size(t) for t in range(1, r)) for r in range(1, rounds)]

    def sum_copy(p, r):
        if r == 0:
            src, dst = part.at[p, pl.ds(bases(0)[1], size(0))], sums.at[p]
        else:
            rows = pl.ds(code_at[r], size(r))
            src, dst = code_out.at[p, rows], code_in.at[p, rows]
        return remote(src, dst, s_send.at[p, r], s_recv.at[p, r], aux=flip(r))

    def top_copy(p, r):
        return remote(top_out.at[p, r], top_in.at[p, r], t_send.at[p, r], t_recv.at[p, r], aux=flip(r))

    def amp_copy(p, r):
        keep, _ = bases(r)
        rows = pl.ds(keep, size(r))
        return remote(amps.at[p, rows], amps.at[p, rows], a_send.at[p, r], a_recv.at[p, r], aux=flip(r))

    def left_block(k):
        return held[pl.ds(nearest(k, v, n_virt), 1)].reshape(naux, block)

    def integrals(p, k, s):
        cols = f_ref[...] if s == 0 else partner[s - 1]
        part[p] = lax.dot_general(left_block(k), cols, (((0,), (0,)), ((), ())), preferred_element_type=F32)
        sum_copy(p, 0).start()

    def add(p, r):
        keep, _ = bases(r)
        sum_copy(p, r).wait_recv()
        rows = pl.ds(keep, size(r))
        if r == 0:
            part[p, rows] = part[p, rows] + sums[p]
        else:
            top_copy(p, r).wait_recv()
            part[p, rows] = part[p, rows] + decode(code_in[p, pl.ds(code_at[r], size(r))], top_in[p, r, :1, :1])
        if r + 1 < rounds:
            _, give = bases(r + 1)
            x = part[p, pl.ds(give, size(r + 1))]
            top = jnp.maximum(jnp.max(jnp.abs(x), axis=(0, 1), keepdims=True), 1e-30)
            top_out[p, r + 1] = jnp.broadcast_to(top, top_out.shape[2:])
            code_out[p, pl.ds(code_at[r + 1], size(r + 1))] = encode(x, top)
            top_copy(p, r + 1).start()
            sum_copy(p, r + 1).start()

    def amplitudes(p, k, s):
        keep, _ = bases(rounds - 1)
        rows = pl.ds(keep, size(rounds - 1))
        gap = er_ref[pl.ds(nearest(k, v, n_virt), 1)].reshape(size(rounds - 1), 1) + ec_ref[s : s + 1]
        amps[p, rows] = (part[p, rows] / gap).astype(BF16)
        amp_copy(p, rounds - 1).start()

    def spread(p, r):
        amp_copy(p, r).wait_recv()
        if r > 0:
            amp_copy(p, r - 1).start()

    def contract(p, k, s):
        term = lax.dot_general(left_block(k), amps[p], (((1,), (0,)), ((), ())), preferred_element_type=F32)
        if k == 0:
            dens[s] = term
        else:
            dens[s] = dens[s] + term

    def back(s):
        return remote(
            dsend.at[s - 1], drecv.at[s - 1], d_send.at[s - 1], d_recv.at[s - 1], occ=lax.rem(o + s, n_occ)
        )

    groups = [[(0, 0)]]
    groups.append([(0, s) for s in range(1, steps)])
    for k in range(1, n_virt):
        pieces = [(k, s) for s in reversed(range(steps))]
        if k == 1:
            groups[1] += pieces
        else:
            groups.append(pieces)

    def finish(p, k, s):
        for r in reversed(range(rounds)):
            spread(p, r)
        contract(p, k, s)
        if k == n_virt - 1 and s > 0:
            dsend[s - 1] = dens[s].astype(BF16)
            back(s).start()

    number = 0
    before = []
    for g, group in enumerate(groups):
        if g > 0:
            for h in range(HALVES):
                arrive(g, h)
        if g == 1:
            for s in range(1, steps):
                across(s).wait_recv()
        named = []
        for k, s in group:
            named.append((number, k, s))
            number += 1
        last = g == len(groups) - 1
        for p, k, s in named:
            integrals(p, k, s)
            for q in before[:1]:
                finish(*q)
            before = before[1:]
        for p, k, s in named:
            add(p, 0)
        for q in before:
            finish(*q)
        for r in range(1, rounds):
            for p, k, s in named:
                add(p, r)
                if r == rounds - 1:
                    amplitudes(p, k, s)
                    if last:
                        finish(p, k, s)
        before = [] if last else named

    out_ref[...] = dens[0]
    for s in range(1, steps):
        back(s).wait_recv()
        out_ref[...] += drecv[s - 1].astype(F32)

    for s in range(1, steps):
        back(s).wait_send()
        across(s).wait_send()
    for p in range(number):
        for r in range(rounds):
            sum_copy(p, r).wait_send()
            if r > 0:
                top_copy(p, r).wait_send()
            amp_copy(p, r).wait_send()
    for k in range(n_virt - 1):

        @pl.when((v >= k) & has_right)
        def _():
            for h in range(HALVES):
                along(held.at[v - k], v - k, h, True).wait_send()

        @pl.when((v + k <= n_virt - 1) & has_left)
        def _():
            for h in range(HALVES):
                along(held.at[v + k], v + k, h, False).wait_send()


def on_device(sizes, factors, occ_energy, virt_energy):
    n_occ, n_virt, n_aux = sizes
    steps = min(WINDOW, n_occ)
    naux, occ_width, virt_width = factors.shape
    block = occ_width * virt_width
    rounds = n_aux.bit_length() - 1
    rows = block // n_aux
    o, v, u = (lax.axis_index(name) for name in AXES)

    eo = occ_energy.reshape(n_occ, occ_width)
    ev = virt_energy.reshape(n_virt, virt_width)
    eo_own = lax.dynamic_index_in_dim(eo, o, 0, keepdims=False)
    er = (eo_own[None, :, None] - ev[:, None, :]).reshape(n_virt, block)
    first = 0
    for r in range(rounds):
        first = first + ((u >> r) & 1) * (block >> (r + 1))
    er = lax.dynamic_slice_in_dim(er, first, rows, 1).reshape(n_virt, rows, 1)
    ev_own = lax.dynamic_index_in_dim(ev, v, 0, keepdims=False)
    eo_cols = jnp.roll(eo, -o, 0)[:steps]
    ec = (eo_cols[:, :, None] - ev_own[None, None, :]).reshape(steps, block)

    pieces = n_virt * steps
    dma = pltpu.SemaphoreType.DMA
    flops = 4 * pieces * naux * block * block
    density = pl.pallas_call(
        functools.partial(kernel, n_occ, n_virt, n_aux, steps),
        out_shape=jax.ShapeDtypeStruct((naux, block), F32),
        in_specs=[pl.BlockSpec(memory_space=pltpu.VMEM)] * 3,
        out_specs=pl.BlockSpec(memory_space=pltpu.VMEM),
        scratch_shapes=[
            pltpu.VMEM((n_virt, naux, block), BF16),
            pltpu.VMEM((steps - 1, naux, block), BF16),
            pltpu.VMEM((pieces, block, block), F32),
            pltpu.VMEM((pieces, block // 2, block), F32),
            pltpu.VMEM((pieces, block // 2 - rows, block), BF16),
            pltpu.VMEM((pieces, block // 2 - rows, block), BF16),
            pltpu.VMEM((pieces, rounds, 8, 128), F32),
            pltpu.VMEM((pieces, rounds, 8, 128), F32),
            pltpu.VMEM((pieces, block, block), BF16),
            pltpu.VMEM((steps, naux, block), F32),
            pltpu.VMEM((steps - 1, naux, block), BF16),
            pltpu.VMEM((steps - 1, naux, block), BF16),
            dma((2, n_virt, HALVES)), dma((n_virt, HALVES)),
            dma((steps - 1,)), dma((steps - 1,)),
            dma((steps - 1,)), dma((steps - 1,)),
            dma((pieces, rounds)), dma((pieces, rounds)),
            dma((pieces, rounds)), dma((pieces, rounds)),
            dma((pieces, rounds)), dma((pieces, rounds)),
        ],
        compiler_params=pltpu.CompilerParams(
            collective_id=0, has_side_effects=True, vmem_limit_bytes=60 << 20
        ),
        cost_estimate=pl.CostEstimate(flops=flops, bytes_accessed=6 * naux * block, transcendentals=0),
    )(factors.reshape(naux, block), er, ec)
    return density.reshape(factors.shape)


def solution(mesh):
    sizes = tuple(mesh.shape[name] for name in AXES)
    return jax.shard_map(
        functools.partial(on_device, sizes),
        mesh=mesh,
        in_specs=(P("aux", "occ", "virt"), P(), P()),
        out_specs=P("aux", "occ", "virt"),
        check_vma=False,
    )
```

```python
import functools

import jax
import jax.numpy as jnp
from jax import lax
from jax.experimental import pallas as pl
from jax.experimental.pallas import tpu as pltpu
from jax.sharding import PartitionSpec as P

AXES = ("occ", "virt", "aux")
WINDOW = 3
HALVES = 2
SPAN = 120.0
F32, BF16 = jnp.float32, jnp.bfloat16


def nearest(k, v, n):
    left, right = v, n - 1 - v
    short = jnp.minimum(left, right)
    alternating = v - (k + 1) // 2 if k % 2 else v + k // 2
    beyond = jnp.where(left <= right, k, n - 1 - k)
    return jnp.where(k <= 2 * short, alternating, beyond)


def encode(x, top):
    z = jnp.exp2(jnp.abs(x) * (2 * SPAN / top) - SPAN)
    return jnp.where(x < 0, -z, z).astype(BF16)


def decode(z, top):
    z = z.astype(F32)
    x = (jnp.log2(jnp.abs(z)) + SPAN) * (top * (0.5 / SPAN))
    return jnp.where(z < 0, -x, x)


def kernel(
    n_occ, n_virt, n_aux, steps,
    f_ref, er_ref, ec_ref, out_ref,
    held, partner, part, sums, code_out, code_in, top_out, top_in, amps, dens, dsend, drecv,
    z_send, z_recv, y_send, y_recv, d_send, d_recv, s_send, s_recv, t_send, t_recv, a_send, a_recv,
):
    o, v, u = (lax.axis_index(name) for name in AXES)
    rounds = n_aux.bit_length() - 1
    naux, block = f_ref.shape
    has_left, has_right = v >= 1, v <= n_virt - 2

    def remote(src, dst, send, recv, **where):
        at = {"occ": o, "virt": v, "aux": u, **where}
        return pltpu.make_async_remote_copy(
            src_ref=src, dst_ref=dst, send_sem=send, recv_sem=recv,
            device_id=tuple(at[name] for name in AXES), device_id_type=pl.DeviceIdType.MESH,
        )

    def flip(r):
        bit = 1 << r
        return u + bit - 2 * bit * (u // bit % 2)

    barrier = pltpu.get_barrier_semaphore()

    def greet(**where):
        at = {"occ": o, "virt": v, "aux": u, **where}
        pl.semaphore_signal(
            barrier, inc=1, device_id=tuple(at[name] for name in AXES), device_id_type=pl.DeviceIdType.MESH
        )

    offsets = sorted({d % n_occ for s in range(1, steps) for d in (s, -s)})
    for d in offsets:
        greet(occ=lax.rem(o + d, n_occ))
    for r in range(rounds):
        greet(aux=flip(r))

    @pl.when(has_left)
    def _():
        greet(virt=v - 1)

    @pl.when(has_right)
    def _():
        greet(virt=v + 1)

    ends = jnp.minimum(v, 1) + jnp.minimum(n_virt - 1 - v, 1)
    pl.semaphore_wait(barrier, len(offsets) + rounds + ends)

    deep = naux // HALVES

    def along(src, w, h, to_right):
        rows = pl.ds(h * deep, deep)
        if to_right:
            return remote(src.at[rows], held.at[w, rows], z_send.at[0, w, h], z_recv.at[w, h], virt=v + 1)
        return remote(src.at[rows], held.at[w, rows], z_send.at[1, w, h], z_recv.at[w, h], virt=v - 1)

    @pl.when(has_right)
    def _():
        for h in range(HALVES):
            along(f_ref, v, h, True).start()

    @pl.when(has_left)
    def _():
        for h in range(HALVES):
            along(f_ref, v, h, False).start()

    def across(s):
        return remote(
            f_ref, partner.at[s - 1], y_send.at[s - 1], y_recv.at[s - 1], occ=lax.rem(o - s + n_occ, n_occ)
        )

    for s in range(1, steps):
        across(s).start()

    held[pl.ds(v, 1)] = f_ref[...].reshape(1, naux, block)

    def arrive(k, h):
        @pl.when(v >= k)
        def _():
            w = v - k
            along(held.at[w], w, h, True).wait_recv()

            @pl.when(has_right)
            def _():
                along(held.at[w], w, h, True).start()

        @pl.when(v + k <= n_virt - 1)
        def _():
            w = v + k
            along(held.at[w], w, h, False).wait_recv()

            @pl.when(has_left)
            def _():
                along(held.at[w], w, h, False).start()

    def size(r):
        return block >> (r + 1)

    def bases(r):
        base = 0
        for t in range(r):
            base = base + (u // (1 << t) % 2) * size(t)
        bit = u // (1 << r) % 2
        keep = pl.multiple_of(base + bit * size(r), size(r))
        give = pl.multiple_of(base + (1 - bit) * size(r), size(r))
        return keep, give

    code_at = [0] + [sum(size(t) for t in range(1, r)) for r in range(1, rounds)]

    def sum_copy(p, r):
        if r == 0:
            src, dst = part.at[p, pl.ds(bases(0)[1], size(0))], sums.at[p]
        else:
            rows = pl.ds(code_at[r], size(r))
            src, dst = code_out.at[p, rows], code_in.at[p, rows]
        return remote(src, dst, s_send.at[p, r], s_recv.at[p, r], aux=flip(r))

    def top_copy(p, r):
        return remote(top_out.at[p, r], top_in.at[p, r], t_send.at[p, r], t_recv.at[p, r], aux=flip(r))

    def amp_copy(p, r):
        keep, _ = bases(r)
        rows = pl.ds(keep, size(r))
        return remote(amps.at[p, rows], amps.at[p, rows], a_send.at[p, r], a_recv.at[p, r], aux=flip(r))

    def left_block(k):
        return held[pl.ds(nearest(k, v, n_virt), 1)].reshape(naux, block)

    def integrals(p, k, s):
        cols = f_ref[...] if s == 0 else partner[s - 1]
        part[p] = lax.dot_general(left_block(k), cols, (((0,), (0,)), ((), ())), preferred_element_type=F32)
        sum_copy(p, 0).start()

    def add(p, r):
        keep, _ = bases(r)
        sum_copy(p, r).wait_recv()
        rows = pl.ds(keep, size(r))
        if r == 0:
            part[p, rows] = part[p, rows] + sums[p]
        else:
            top_copy(p, r).wait_recv()
            part[p, rows] = part[p, rows] + decode(code_in[p, pl.ds(code_at[r], size(r))], top_in[p, r, :1, :1])
        if r + 1 < rounds:
            _, give = bases(r + 1)
            x = part[p, pl.ds(give, size(r + 1))]
            top = jnp.maximum(jnp.max(jnp.abs(x), axis=(0, 1), keepdims=True), 1e-30)
            top_out[p, r + 1] = jnp.broadcast_to(top, top_out.shape[2:])
            code_out[p, pl.ds(code_at[r + 1], size(r + 1))] = encode(x, top)
            top_copy(p, r + 1).start()
            sum_copy(p, r + 1).start()

    def amplitudes(p, k, s):
        keep, _ = bases(rounds - 1)
        rows = pl.ds(keep, size(rounds - 1))
        gap = er_ref[pl.ds(nearest(k, v, n_virt), 1)].reshape(size(rounds - 1), 1) + ec_ref[s : s + 1]
        amps[p, rows] = (part[p, rows] / gap).astype(BF16)
        amp_copy(p, rounds - 1).start()

    def spread(p, r):
        amp_copy(p, r).wait_recv()
        if r > 0:
            amp_copy(p, r - 1).start()

    def contract(p, k, s):
        term = lax.dot_general(left_block(k), amps[p], (((1,), (0,)), ((), ())), preferred_element_type=F32)
        if k == 0:
            dens[s] = term
        else:
            dens[s] = dens[s] + term

    def back(s, h):
        rows = pl.ds(h * deep, deep)
        return remote(
            dsend.at[s - 1, rows], drecv.at[s - 1, rows], d_send.at[s - 1, h], d_recv.at[s - 1, h],
            occ=lax.rem(o + s, n_occ),
        )

    groups = [[(0, 0)]]
    groups.append([(0, s) for s in range(1, steps)])
    for k in range(1, n_virt):
        pieces = [(k, s) for s in reversed(range(steps))]
        if k == 1:
            groups[1] += pieces
        else:
            groups.append(pieces)

    def finish(p, k, s):
        for r in reversed(range(rounds)):
            spread(p, r)
        if k < n_virt - 1 or s == 0:
            contract(p, k, s)
            return
        for h in range(HALVES):
            rows = pl.ds(h * deep, deep)
            left = held[pl.ds(nearest(k, v, n_virt), 1), rows].reshape(deep, block)
            term = lax.dot_general(left, amps[p], (((1,), (0,)), ((), ())), preferred_element_type=F32)
            dsend[s - 1, rows] = (dens[s, rows] + term).astype(BF16)
            back(s, h).start()

    number = 0
    before = []
    for g, group in enumerate(groups):
        if g > 0:
            for h in range(HALVES):
                arrive(g, h)
        if g == 1:
            for s in range(1, steps):
                across(s).wait_recv()
        named = []
        for k, s in group:
            named.append((number, k, s))
            number += 1
        last = g == len(groups) - 1
        if not last:
            for p, k, s in named:
                integrals(p, k, s)
                for q in before[:1]:
                    finish(*q)
                before = before[1:]
            for p, k, s in named:
                add(p, 0)
            for q in before:
                finish(*q)
            for r in range(1, rounds):
                for p, k, s in named:
                    add(p, r)
                    if r == rounds - 1:
                        amplitudes(p, k, s)
            before = named
            continue
        for piece in named[:-1]:
            integrals(*piece)
        for piece in named[:-1]:
            add(piece[0], 0)
        for q in before:
            finish(*q)
        for r in range(1, rounds):
            for piece in named[:-1]:
                add(piece[0], r)
        for piece in named[:-1]:
            amplitudes(*piece)
        integrals(*named[-1])
        add(named[-1][0], 0)
        for piece in named[:-1]:
            finish(*piece)
        for r in range(1, rounds):
            add(named[-1][0], r)
        amplitudes(*named[-1])
        finish(*named[-1])

    for h in range(HALVES):
        rows = pl.ds(h * deep, deep)
        total = dens[0, rows]
        for s in range(1, steps):
            back(s, h).wait_recv()
            total = total + drecv[s - 1, rows].astype(F32)
        out_ref[rows] = total

    for s in range(1, steps):
        for h in range(HALVES):
            back(s, h).wait_send()
        across(s).wait_send()
    for p in range(number):
        for r in range(rounds):
            sum_copy(p, r).wait_send()
            if r > 0:
                top_copy(p, r).wait_send()
            amp_copy(p, r).wait_send()
    for k in range(n_virt - 1):

        @pl.when((v >= k) & has_right)
        def _():
            for h in range(HALVES):
                along(held.at[v - k], v - k, h, True).wait_send()

        @pl.when((v + k <= n_virt - 1) & has_left)
        def _():
            for h in range(HALVES):
                along(held.at[v + k], v + k, h, False).wait_send()


def on_device(sizes, factors, occ_energy, virt_energy):
    n_occ, n_virt, n_aux = sizes
    steps = min(WINDOW, n_occ)
    naux, occ_width, virt_width = factors.shape
    block = occ_width * virt_width
    rounds = n_aux.bit_length() - 1
    rows = block // n_aux
    o, v, u = (lax.axis_index(name) for name in AXES)

    eo = occ_energy.reshape(n_occ, occ_width)
    ev = virt_energy.reshape(n_virt, virt_width)
    eo_own = lax.dynamic_index_in_dim(eo, o, 0, keepdims=False)
    er = (eo_own[None, :, None] - ev[:, None, :]).reshape(n_virt, block)
    first = 0
    for r in range(rounds):
        first = first + ((u >> r) & 1) * (block >> (r + 1))
    er = lax.dynamic_slice_in_dim(er, first, rows, 1).reshape(n_virt, rows, 1)
    ev_own = lax.dynamic_index_in_dim(ev, v, 0, keepdims=False)
    eo_cols = jnp.roll(eo, -o, 0)[:steps]
    ec = (eo_cols[:, :, None] - ev_own[None, None, :]).reshape(steps, block)

    pieces = n_virt * steps
    dma = pltpu.SemaphoreType.DMA
    flops = 4 * pieces * naux * block * block
    density = pl.pallas_call(
        functools.partial(kernel, n_occ, n_virt, n_aux, steps),
        out_shape=jax.ShapeDtypeStruct((naux, block), F32),
        in_specs=[pl.BlockSpec(memory_space=pltpu.VMEM)] * 3,
        out_specs=pl.BlockSpec(memory_space=pltpu.VMEM),
        scratch_shapes=[
            pltpu.VMEM((n_virt, naux, block), BF16),
            pltpu.VMEM((steps - 1, naux, block), BF16),
            pltpu.VMEM((pieces, block, block), F32),
            pltpu.VMEM((pieces, block // 2, block), F32),
            pltpu.VMEM((pieces, block // 2 - rows, block), BF16),
            pltpu.VMEM((pieces, block // 2 - rows, block), BF16),
            pltpu.VMEM((pieces, rounds, 8, 128), F32),
            pltpu.VMEM((pieces, rounds, 8, 128), F32),
            pltpu.VMEM((pieces, block, block), BF16),
            pltpu.VMEM((steps, naux, block), F32),
            pltpu.VMEM((steps - 1, naux, block), BF16),
            pltpu.VMEM((steps - 1, naux, block), BF16),
            dma((2, n_virt, HALVES)), dma((n_virt, HALVES)),
            dma((steps - 1,)), dma((steps - 1,)),
            dma((steps - 1, HALVES)), dma((steps - 1, HALVES)),
            dma((pieces, rounds)), dma((pieces, rounds)),
            dma((pieces, rounds)), dma((pieces, rounds)),
            dma((pieces, rounds)), dma((pieces, rounds)),
        ],
        compiler_params=pltpu.CompilerParams(
            collective_id=0, has_side_effects=True, vmem_limit_bytes=60 << 20
        ),
        cost_estimate=pl.CostEstimate(flops=flops, bytes_accessed=6 * naux * block, transcendentals=0),
    )(factors.reshape(naux, block), er, ec)
    return density.reshape(factors.shape)


def solution(mesh):
    sizes = tuple(mesh.shape[name] for name in AXES)
    return jax.shard_map(
        functools.partial(on_device, sizes),
        mesh=mesh,
        in_specs=(P("aux", "occ", "virt"), P(), P()),
        out_specs=P("aux", "occ", "virt"),
        check_vma=False,
    )
```
